32 devices in a mesh: member: 1, lat: 4 (over z), lev: 4 (over y, x), fld: 2 (over core).
Axes of the slice: x: 2, y: 2, z: 4, core: 2. Of those that a mesh axis runs over, the one named last changes fastest.
Arguments:
- grid_state: bfloat16 [2, 16, 2, 512, 2048], P('member', 'lev', 'fld', 'lat'), may hold values from -6 to 6
- legendre: bfloat16 [512, 2, 512, 640], P(('lat', 'lev'), 'fld'), may hold values from -0.25 to 0.25
- pair_order: int32 [512], replicated, may hold values from 0 to 511, each once
- band_start: int32 [1024], replicated, may hold values from 0 to 286
- mode_analysis: float32 [32, 32], replicated, may hold values from -1 to 1
- mode_synthesis: float32 [32, 32], replicated, may hold values from -1 to 1
- mode_rate: float32 [32], replicated, may hold values from 0.05 to 50
Outputs:
- grid_out: bfloat16 [2, 16, 2, 512, 2048], P('member', 'lev', 'fld', 'lat')
The draws below stay inside these ranges and needn't reach their ends.
Inputs may be any that keep to these rules, and one draw needn't show every extreme that they name: `pair_order`: every value appears once.
All inputs are finite; a program needn't handle non-finite values.
Results may differ from the reference program's by a relative error of at most 0.009.
Values may be sent and summed in bfloat16 or wider, within the bound.
A program may use at most 128 MiB of HBM per device.

```python
import math
import jax
import jax.numpy as jnp
from jax import lax

M = 1024
LEVELS = 16
FIELDS = 2
HLAT = 512
NLON = 2048
PAIRS = 512
COLS = 640
MODES = 32


def draw_band_start(key, part):
    wave_list = jnp.arange(M, dtype=jnp.int32)
    spread = jax.random.randint(key, (M,), 0, HLAT // 16, dtype=jnp.int32)
    spread = jnp.where(wave_list == 0, 0, jnp.where(wave_list == M - 1, HLAT // 16 - 1, spread))
    return (wave_list * (HLAT // 2) // M + spread).astype(jnp.int32)


def levels(stream_key, shape, pieces, least, largest):
    def one(axis_at, shards_of):
        steps = jax.random.uniform(jax.random.fold_in(jax.random.fold_in(stream_key, 6), axis_at), (shards_of,), jnp.float32, least / len(pieces), largest / len(pieces))
        return jnp.repeat(jnp.exp(steps), shape[axis_at] // shards_of).reshape((-1,) + (1,) * (len(shape) - axis_at - 1))

    level = one(*pieces[0])
    for cut in pieces[1:]:
        level = level * one(*cut)
    return level


def gaussian(key, shape, deviation, most, shards=(), kind=jnp.bfloat16):
    loudness = levels(key, shape, shards, -0.22, 0.18) if shards else 1.0
    entries = jax.random.normal(key, shape, jnp.float32) * deviation * loudness
    return jnp.minimum(jnp.maximum(entries, -most), most).astype(kind)


def setup_inputs(seed: int = 0, part: int = 0) -> dict:
    streams_of = jax.random.split(jax.random.key(seed), 8)
    own_keys = jax.random.split(jax.random.fold_in(streams_of[7], part), 8)
    grid_state = gaussian(own_keys[0], (2, LEVELS, 2, HLAT, NLON), 1.0, 6.0, ((1, 4), (2, 2), (3, 4)))
    legendre = gaussian(streams_of[1], (PAIRS, 2, HLAT, COLS), HLAT ** -0.5, 0.25, ((0, 16), (1, 2)))
    pair_order = jax.random.permutation(streams_of[2], PAIRS).astype(jnp.int32)
    band_start = draw_band_start(jax.random.fold_in(streams_of[7], 71), part)
    mode_analysis = gaussian(streams_of[4], (MODES, MODES), MODES ** -0.5, 1.0, (), jnp.float32)
    mode_synthesis = gaussian(streams_of[5], (MODES, MODES), MODES ** -0.5, 1.0, (), jnp.float32)
    mode_rate = jnp.clip(jnp.exp(jax.random.uniform(streams_of[6], (MODES,), jnp.float32, math.log(0.05), math.log(50.0))), 0.05, 50.0)
    return {"grid_state": grid_state, "legendre": legendre, "pair_order": pair_order, "band_start": band_start, "mode_analysis": mode_analysis, "mode_synthesis": mode_synthesis, "mode_rate": mode_rate}


def fourier_table(wave_list, lon_count):
    longitude = jnp.arange(lon_count, dtype=jnp.int32)
    phase = longitude[:, None] * wave_list[None, :] % lon_count
    angle = phase.astype(jnp.float32) * jnp.float32(2.0 * math.pi / lon_count)
    scaling = jnp.float32(1.0 / math.sqrt(lon_count))
    return jnp.stack([jnp.cos(angle) * scaling, -jnp.sin(angle) * scaling], axis=1).astype(jnp.bfloat16)

def column_maps(first_wave, parity, wave_count, col_count):
    column = jnp.arange(col_count, dtype=jnp.int32)[None, :]
    first_col = first_wave[:, None]
    second_col = wave_count - 1 - first_col
    count_one = (wave_count - 1 - first_col - parity) // 2 + 1
    count_two = jnp.maximum((first_col - parity) // 2 + 1, 0)
    in_first = column < count_one
    degree = jnp.where(in_first, first_col + parity + 2 * column, second_col + parity + 2 * (column - count_one))
    valid = column < count_one + count_two
    return (in_first, degree, valid)

def mode_factor(degree, mode_rate, wave_count):
    level_deg = degree.astype(jnp.float32)
    growth = level_deg * (level_deg + 1.0) / float(wave_count * wave_count)
    return 1.0 / (1.0 + growth[..., None, :] * mode_rate[:, None])

def reference(grid_state, legendre, pair_order, band_start, mode_analysis, mode_synthesis, mode_rate):
    wind_part = grid_state[0].astype(jnp.float32)
    heat_part = grid_state[1].astype(jnp.float32)
    products = jnp.stack([wind_part * heat_part, wind_part * wind_part - heat_part * heat_part]).astype(jnp.bfloat16)
    products = lax.optimization_barrier(products)
    wave_list = jnp.arange(M, dtype=jnp.int32)
    lon_table = fourier_table(wave_list, NLON)
    grid_rows = products.reshape(-1, NLON).astype(jnp.float32)
    fourier = jnp.dot(grid_rows, lon_table.reshape(NLON, 2 * M).astype(jnp.float32)).astype(jnp.bfloat16)
    fourier = lax.optimization_barrier(fourier)
    fourier = fourier.reshape(FIELDS, LEVELS, 2, HLAT, 2, M).astype(jnp.float32)
    halves = jnp.stack([fourier[:, :, 0] + fourier[:, :, 1], fourier[:, :, 0] - fourier[:, :, 1]]).astype(jnp.bfloat16)
    halves = lax.optimization_barrier(halves)
    by_wave = jnp.transpose(halves, (5, 0, 4, 1, 2, 3))
    latitude = jnp.arange(HLAT, dtype=jnp.int32)

    def one_slot(slot_item):
        slot_table, first_wave = slot_item
        second_wave = M - 1 - first_wave
        results = []
        for parity in range(2):
            in_first, degree, valid = column_maps(first_wave[None], parity, M, COLS)
            start_col = jnp.where(in_first[0], band_start[first_wave], band_start[second_wave])
            keep_mask = valid[0][None, :] & (latitude[:, None] >= start_col[None, :])
            active = jnp.where(keep_mask, slot_table[parity], jnp.zeros((), jnp.bfloat16)).astype(jnp.float32)
            first_part = by_wave[first_wave, parity].astype(jnp.float32)
            second_part = by_wave[second_wave, parity].astype(jnp.float32)
            spec_one = jnp.einsum('eflj,jc->eflc', first_part, active)
            spec_two = jnp.einsum('eflj,jc->eflc', second_part, active)
            spectral = jnp.where(in_first[0], spec_one, spec_two).reshape(2, MODES, COLS)
            mixed = jnp.einsum('ki,eic->ekc', mode_analysis, spectral, precision=lax.Precision.HIGHEST)
            factor = mode_factor(degree, mode_rate, M)[0]
            coupled = jnp.einsum('ik,ekc->eic', mode_synthesis, mixed * factor[None], precision=lax.Precision.HIGHEST)
            coupled = lax.optimization_barrier(coupled.astype(jnp.bfloat16)).astype(jnp.float32)
            coupled = coupled.reshape(2, FIELDS, LEVELS, COLS)
            pick_first = in_first[0].astype(jnp.float32)
            back_one = jnp.einsum('jc,eflc->eflj', active, coupled * pick_first)
            back_two = jnp.einsum('jc,eflc->eflj', active, coupled * (1.0 - pick_first))
            results.append(jnp.stack([back_one, back_two]))
        return jnp.stack(results).astype(jnp.bfloat16)
    per_slot = lax.map(one_slot, (legendre, pair_order))
    slot_of = jnp.zeros((PAIRS,), jnp.int32).at[pair_order].set(jnp.arange(PAIRS, dtype=jnp.int32))
    low_half = per_slot[slot_of][:, :, 0]
    high_half = per_slot[slot_of[::-1]][:, :, 1]
    back_waves = jnp.concatenate([low_half, high_half], axis=0).astype(jnp.float32)
    north_half = back_waves[:, 0] + back_waves[:, 1]
    south_half = back_waves[:, 0] - back_waves[:, 1]
    hemi_grid = jnp.stack([north_half, south_half], axis=0).astype(jnp.bfloat16)
    hemi_grid = lax.optimization_barrier(hemi_grid)
    hemi_grid = jnp.transpose(hemi_grid, (3, 4, 0, 5, 2, 1))
    weight = jnp.where(wave_list == 0, 1.0, 2.0).astype(jnp.float32)
    inverse = (lon_table.astype(jnp.float32) * weight[None, None, :]).astype(jnp.bfloat16)
    grid_out = jnp.dot(hemi_grid.reshape(-1, 2 * M).astype(jnp.float32), inverse.reshape(NLON, 2 * M).astype(jnp.float32).T)
    return grid_out.astype(jnp.bfloat16).reshape(FIELDS, LEVELS, 2, HLAT, NLON)
```

```python
import functools
import math

import jax
import jax.numpy as jnp
from jax import lax
from jax.experimental import pallas as pl
from jax.experimental.pallas import tpu as pltpu
from jax.sharding import PartitionSpec as P

CHUNKS = 2
LANES = 128
F32 = jnp.float32
BF16 = jnp.bfloat16


def swap_pair(value, axis):
    pairs = [(source, source ^ 1) for source in range(lax.axis_size(axis))]
    return lax.ppermute(value, axis, pairs)


def fourier_rows(waves, lon_count):
    unit = F32(2.0 * math.pi / lon_count)
    scaling = F32(1.0 / math.sqrt(lon_count))
    coarse = jnp.arange(lon_count // LANES, dtype=jnp.int32) * LANES
    fine = jnp.arange(LANES, dtype=jnp.int32)
    coarse_angle = (waves[..., None] * coarse % lon_count).astype(F32) * unit
    fine_angle = (waves[..., None] * fine % lon_count).astype(F32) * unit
    cos_a, sin_a = jnp.cos(coarse_angle) * scaling, jnp.sin(coarse_angle) * scaling
    by_cos = jnp.stack([cos_a, -sin_a], axis=1)
    by_sin = jnp.stack([-sin_a, -cos_a], axis=1)
    cos_b, sin_b = jnp.cos(fine_angle)[:, None], jnp.sin(fine_angle)[:, None]
    by_cos, by_sin, cos_b, sin_b = lax.optimization_barrier((by_cos, by_sin, cos_b, sin_b))
    table = by_cos[..., None] * cos_b[..., None, :] + by_sin[..., None] * sin_b[..., None, :]
    return table.astype(BF16).reshape(-1, lon_count)


def slot_kernel(wave_count, first_ref, start_one_ref, start_two_ref, parity_ref,
                x_ref, table_ref, analysis_ref, synthesis_ref, rate_ref, y_ref):
    slot = pl.program_id(0)
    parity = parity_ref[0]
    first = first_ref[slot]
    lat_total, col_count = table_ref.shape[2:]
    half = x_ref.shape[1] // 2
    second = wave_count - 1 - first
    count_one = (second - parity) // 2 + 1
    count_two = jnp.where(first >= parity, (first - parity) // 2 + 1, 0)
    column = lax.broadcasted_iota(jnp.int32, (1, col_count), 1)
    in_first = column < count_one
    degree = jnp.where(in_first, first + parity + 2 * column, second + parity + 2 * (column - count_one))
    start = jnp.where(in_first, start_one_ref[slot], start_two_ref[slot])
    start = jnp.where(column < count_one + count_two, start, lat_total)
    latitude = lax.broadcasted_iota(jnp.int32, (lat_total, col_count), 0)
    active = jnp.where(latitude >= start, table_ref[0, 0].astype(F32), 0.0).astype(BF16)
    both = jnp.dot(x_ref[0], active, preferred_element_type=F32)
    spectral = jnp.where(in_first, both[:half], both[half:])
    level_deg = degree.astype(F32)
    growth = level_deg * (level_deg + 1.0) / float(wave_count * wave_count)
    factor = 1.0 / (1.0 + growth * rate_ref[...])
    mixed = jnp.dot(analysis_ref[...], spectral, precision=lax.Precision.HIGHEST, preferred_element_type=F32)
    coupled = jnp.dot(
        synthesis_ref[...], mixed * factor, precision=lax.Precision.HIGHEST, preferred_element_type=F32
    )
    split = jnp.concatenate([jnp.where(in_first, coupled, 0.0), jnp.where(in_first, 0.0, coupled)]).astype(BF16)
    y_ref[0] = lax.dot_general(
        split, active, (((1,), (1,)), ((), ())), preferred_element_type=F32
    ).astype(BF16)


def local(grid_state, legendre, pair_order, band_start, mode_analysis, mode_synthesis, mode_rate):
    lat_count = lax.axis_size("lat")
    lev_count = lax.axis_size("lev")
    owners = lat_count * lev_count
    owner_index = lax.axis_index("lat") * lev_count + lax.axis_index("lev")
    parity = lax.axis_index("fld")
    wave_count = band_start.shape[0]
    field_count, levels_here, _, lats_here, lon_count = grid_state.shape
    slots_here, _, lat_total, col_count = legendre.shape
    modes_count = mode_rate.shape[0]
    chunks = CHUNKS if slots_here % CHUNKS == 0 else 1
    size = slots_here // chunks
    rows = 4 * modes_count
    wind, heat = grid_state[0].astype(F32), grid_state[1].astype(F32)
    products = jnp.stack([wind * heat, wind * wind - heat * heat]).astype(BF16)
    grid_rows = products.reshape(-1, lon_count)
    sign_own = (1 - 2 * parity).astype(F32)
    slot_waves = jnp.stack([pair_order, wave_count - 1 - pair_order], axis=1)
    slot_waves = slot_waves.reshape(owners, chunks, size * 2)

    first_wave = lax.dynamic_slice_in_dim(pair_order, owner_index * slots_here, slots_here)
    second_wave = wave_count - 1 - first_wave
    wave_index = jnp.arange(wave_count, dtype=jnp.int32)[None, :]
    start_one = jnp.sum(jnp.where(wave_index == first_wave[:, None], band_start[None, :], 0), axis=1)
    start_two = jnp.sum(jnp.where(wave_index == second_wave[:, None], band_start[None, :], 0), axis=1)
    eye = jnp.eye(2, dtype=F32)
    double = lambda matrix: (eye[:, None, :, None] * matrix[None, :, None, :]).reshape(
        2 * modes_count, 2 * modes_count
    )
    analysis, synthesis = double(mode_analysis), double(mode_synthesis)
    rate = jnp.concatenate([mode_rate, mode_rate])[:, None]
    parity_arg = parity.astype(jnp.int32).reshape(1)

    tables, arrived = [], []
    for chunk in range(chunks):
        table = fourier_rows(slot_waves[:, chunk], lon_count)
        table = lax.optimization_barrier(table)
        tables.append(table)
        fourier = lax.dot_general(
            table, grid_rows, (((1,), (1,)), ((), ())), preferred_element_type=F32
        ).astype(BF16)
        mirror = swap_pair(fourier, "fld")
        halves = (mirror.astype(F32) + sign_own * fourier.astype(F32)).astype(BF16)
        halves = halves.reshape(owners, 2 * size * 2, -1)
        arrived.append(lax.all_to_all(halves, ("lat", "lev"), split_axis=0, concat_axis=0, tiled=True))

    returned = []
    for chunk in range(chunks):
        part = arrived[chunk].reshape(
            lat_count, lev_count, 2, size, 2, field_count, levels_here, lats_here
        )
        part = part.transpose(3, 4, 2, 5, 1, 6, 0, 7).reshape(size, rows, lat_total)
        whole = lambda shape: pl.BlockSpec(shape, lambda i, *_: (0,) * len(shape))
        back = pl.pallas_call(
            functools.partial(slot_kernel, wave_count),
            out_shape=jax.ShapeDtypeStruct((size, rows, lat_total), BF16),
            grid_spec=pltpu.PrefetchScalarGridSpec(
                num_scalar_prefetch=4,
                grid=(size,),
                in_specs=[
                    pl.BlockSpec((1, rows, lat_total), lambda i, *_: (i, 0, 0)),
                    pl.BlockSpec(
                        (1, 1, lat_total, col_count),
                        functools.partial(lambda base, i, *_: (base + i, 0, 0, 0), chunk * size),
                    ),
                    whole(analysis.shape),
                    whole(synthesis.shape),
                    whole(rate.shape),
                ],
                out_specs=pl.BlockSpec((1, rows, lat_total), lambda i, *_: (i, 0, 0)),
            ),
            compiler_params=pltpu.CompilerParams(vmem_limit_bytes=24 * 2**20),
            cost_estimate=pl.CostEstimate(
                flops=size * 4 * rows * lat_total * col_count * 4,
                bytes_accessed=size * 2 * (lat_total * col_count + 2 * rows * lat_total),
                transcendentals=0,
            ),
        )(
            first_wave[chunk * size:(chunk + 1) * size],
            start_one[chunk * size:(chunk + 1) * size],
            start_two[chunk * size:(chunk + 1) * size],
            parity_arg, part, legendre, analysis, synthesis, rate,
        )
        back = back.reshape(size, 2, 2, field_count, lev_count, levels_here, lat_count, lats_here)
        back = back.transpose(6, 4, 2, 0, 1, 3, 5, 7).reshape(owners, 2 * size * 2, -1)
        returned.append(lax.all_to_all(back, ("lat", "lev"), split_axis=0, concat_axis=0, tiled=True))

    total = None
    for chunk in range(chunks):
        own = returned[chunk].reshape(owners, 2, size * 2, -1)
        partner = swap_pair(own, "fld")
        weight = jnp.where(slot_waves[:, chunk] == 0, 1.0, 2.0).astype(F32)
        hemisphere = (partner.astype(F32) + sign_own * own.astype(F32)) * weight[:, None, :, None]
        hemisphere = hemisphere.astype(BF16).reshape(owners * 4 * size, -1)
        term = lax.dot_general(
            hemisphere, tables[chunk], (((0,), (0,)), ((), ())), preferred_element_type=F32
        )
        total = term if total is None else total + term
    return total.astype(BF16).reshape(field_count, levels_here, 1, lats_here, lon_count)


def solution(mesh):
    return jax.shard_map(
        local,
        mesh=mesh,
        in_specs=(
            P("member", "lev", "fld", "lat", None),
            P(("lat", "lev"), "fld", None, None),
            P(),
            P(),
            P(),
            P(),
            P(),
        ),
        out_specs=P("member", "lev", "fld", "lat", None),
        check_vma=False,
    )
```

```python
import functools
import math

import jax
import jax.numpy as jnp
from jax import lax
from jax.experimental import pallas as pl
from jax.experimental.pallas import tpu as pltpu
from jax.sharding import PartitionSpec as P

SHARES = (1, 1)
LANES = 128
F32 = jnp.float32
BF16 = jnp.bfloat16


def swap_pair(value, axis):
    pairs = [(source, source ^ 1) for source in range(lax.axis_size(axis))]
    return lax.ppermute(value, axis, pairs)


def fourier_rows(waves, lon_count):
    unit = F32(2.0 * math.pi / lon_count)
    scaling = F32(1.0 / math.sqrt(lon_count))
    coarse = jnp.arange(lon_count // LANES, dtype=jnp.int32) * LANES
    fine = jnp.arange(LANES, dtype=jnp.int32)
    coarse_angle = (waves[..., None] * coarse % lon_count).astype(F32) * unit
    fine_angle = (waves[..., None] * fine % lon_count).astype(F32) * unit
    cos_a, sin_a = jnp.cos(coarse_angle) * scaling, jnp.sin(coarse_angle) * scaling
    by_cos = jnp.stack([cos_a, -sin_a], axis=1)
    by_sin = jnp.stack([-sin_a, -cos_a], axis=1)
    cos_b, sin_b = jnp.cos(fine_angle), jnp.sin(fine_angle)
    cos_b, sin_b = jnp.stack([cos_b, cos_b], axis=1), jnp.stack([sin_b, sin_b], axis=1)
    parts = [part.reshape(-1, part.shape[-1]) for part in (by_cos, by_sin, cos_b, sin_b)]
    count = parts[0].shape[0]
    block = math.gcd(count, 256)
    return pl.pallas_call(
        table_kernel,
        out_shape=jax.ShapeDtypeStruct((count, lon_count), BF16),
        grid=(count // block,),
        in_specs=[pl.BlockSpec((block, part.shape[1]), lambda i: (i, 0)) for part in parts],
        out_specs=pl.BlockSpec((block, lon_count), lambda i: (i, 0)),
        compiler_params=pltpu.CompilerParams(vmem_limit_bytes=8 * 2**20),
        cost_estimate=pl.CostEstimate(flops=3 * count * lon_count, bytes_accessed=2 * count * lon_count, transcendentals=0),
    )(*parts)


def table_kernel(cos_a_ref, sin_a_ref, cos_b_ref, sin_b_ref, out_ref):
    cos_b, sin_b = cos_b_ref[...], sin_b_ref[...]
    for step in range(cos_a_ref.shape[1]):
        here = slice(step, step + 1)
        value = cos_a_ref[:, here] * cos_b + sin_a_ref[:, here] * sin_b
        out_ref[:, step * LANES:(step + 1) * LANES] = value.astype(BF16)


def slot_kernel(wave_count, lev_count, first_ref, start_one_ref, start_two_ref, parity_ref,
                x_ref, table_ref, analysis_ref, synthesis_ref, rate_ref, y_ref):
    slot = pl.program_id(0)
    parity = parity_ref[0]
    first = first_ref[slot]
    lat_total, col_count = table_ref.shape[2:]
    owners, _, _, _, fields, lats = x_ref.shape
    lat_count = owners // lev_count
    places = [(w, e, b) for w in range(2) for e in range(2) for b in range(lev_count)]
    x = jnp.concatenate(
        [
            jnp.concatenate([x_ref[a * lev_count + b, e, 0, w].astype(F32) for w, e, b in places], axis=0)
            for a in range(lat_count)
        ],
        axis=1,
    ).astype(BF16)
    half = x.shape[0] // 2
    second = wave_count - 1 - first
    count_one = (second - parity) // 2 + 1
    count_two = jnp.where(first >= parity, (first - parity) // 2 + 1, 0)
    column = lax.broadcasted_iota(jnp.int32, (1, col_count), 1)
    in_first = column < count_one
    degree = jnp.where(in_first, first + parity + 2 * column, second + parity + 2 * (column - count_one))
    start = jnp.where(in_first, start_one_ref[slot], start_two_ref[slot])
    start = jnp.where(column < count_one + count_two, start, lat_total)
    latitude = lax.broadcasted_iota(jnp.int32, (lat_total, col_count), 0)
    active = jnp.where(latitude >= start, table_ref[0, 0].astype(F32), 0.0).astype(BF16)
    both = jnp.dot(x, active, preferred_element_type=F32)
    spectral = jnp.where(in_first, both[:half], both[half:])
    level_deg = degree.astype(F32)
    growth = level_deg * (level_deg + 1.0) / float(wave_count * wave_count)
    factor = 1.0 / (1.0 + growth * rate_ref[...])
    mixed = jnp.dot(analysis_ref[...], spectral, precision=lax.Precision.HIGHEST, preferred_element_type=F32)
    coupled = jnp.dot(
        synthesis_ref[...], mixed * factor, precision=lax.Precision.HIGHEST, preferred_element_type=F32
    )
    split = jnp.concatenate([jnp.where(in_first, coupled, 0.0), jnp.where(in_first, 0.0, coupled)]).astype(BF16)
    y = lax.dot_general(split, active, (((1,), (1,)), ((), ())), preferred_element_type=F32)
    for at, (w, e, b) in enumerate(places):
        for a in range(lat_count):
            y_ref[a * lev_count + b, e, 0, w] = y[
                at * fields:(at + 1) * fields, a * lats:(a + 1) * lats
            ].astype(BF16)


def local(grid_state, legendre, pair_order, band_start, mode_analysis, mode_synthesis, mode_rate):
    lat_count = lax.axis_size("lat")
    lev_count = lax.axis_size("lev")
    owners = lat_count * lev_count
    owner_index = lax.axis_index("lat") * lev_count + lax.axis_index("lev")
    parity = lax.axis_index("fld")
    wave_count = band_start.shape[0]
    field_count, levels_here, _, lats_here, lon_count = grid_state.shape
    slots_here, _, lat_total, col_count = legendre.shape
    modes_count = mode_rate.shape[0]
    shares = SHARES if slots_here % sum(SHARES) == 0 else (1,)
    sizes = [share * slots_here // sum(shares) for share in shares]
    bases = [sum(sizes[:at]) for at in range(len(sizes))]
    chunks = len(sizes)
    fields = field_count * levels_here
    wind, heat = grid_state[0].astype(F32), grid_state[1].astype(F32)
    products = jnp.stack([wind * heat, wind * wind - heat * heat]).astype(BF16)
    grid_rows = products.reshape(-1, lon_count)
    sign_own = (1 - 2 * parity).astype(F32)
    slot_waves = jnp.stack([pair_order, wave_count - 1 - pair_order], axis=1)
    slot_waves = slot_waves.reshape(owners, slots_here * 2)
    chunk_waves = [slot_waves[:, 2 * base:2 * (base + size)] for base, size in zip(bases, sizes)]

    first_wave = lax.dynamic_slice_in_dim(pair_order, owner_index * slots_here, slots_here)
    second_wave = wave_count - 1 - first_wave
    wave_index = jnp.arange(wave_count, dtype=jnp.int32)[None, :]
    start_one = jnp.sum(jnp.where(wave_index == first_wave[:, None], band_start[None, :], 0), axis=1)
    start_two = jnp.sum(jnp.where(wave_index == second_wave[:, None], band_start[None, :], 0), axis=1)
    eye = jnp.eye(2, dtype=F32)
    double = lambda matrix: (eye[:, None, :, None] * matrix[None, :, None, :]).reshape(
        2 * modes_count, 2 * modes_count
    )
    order = jnp.arange(modes_count).reshape(field_count, lev_count, levels_here)
    order = order.transpose(1, 0, 2).reshape(-1)
    analysis, synthesis = double(mode_analysis[:, order]), double(mode_synthesis[order])
    rate = jnp.concatenate([mode_rate, mode_rate])[:, None]
    parity_arg = parity.astype(jnp.int32).reshape(1)

    tables, arrived = [], []
    for chunk in range(chunks):
        table = fourier_rows(chunk_waves[chunk], lon_count)
        tables.append(table)
        fourier = lax.dot_general(
            table, grid_rows, (((1,), (1,)), ((), ())), preferred_element_type=F32
        ).astype(BF16)
        mirror = swap_pair(fourier, "fld")
        halves = (mirror.astype(F32) + sign_own * fourier.astype(F32)).astype(BF16)
        halves = halves.reshape(owners, 4 * sizes[chunk], fields, lats_here)
        arrived.append(lax.all_to_all(halves, ("lat", "lev"), split_axis=0, concat_axis=0, tiled=True))

    returned = []
    for chunk in range(chunks):
        base, size = bases[chunk], sizes[chunk]
        piece = (owners, 2, size, 2, fields, lats_here)
        part = arrived[chunk].reshape(piece)
        whole = lambda shape: pl.BlockSpec(shape, lambda i, *_: (0,) * len(shape))
        back = pl.pallas_call(
            functools.partial(slot_kernel, wave_count, lev_count),
            out_shape=jax.ShapeDtypeStruct(piece, BF16),
            grid_spec=pltpu.PrefetchScalarGridSpec(
                num_scalar_prefetch=4,
                grid=(size,),
                in_specs=[
                    pl.BlockSpec((owners, 2, 1, 2, fields, lats_here), lambda i, *_: (0, 0, i, 0, 0, 0)),
                    pl.BlockSpec(
                        (1, 1, lat_total, col_count),
                        functools.partial(lambda base, i, *_: (base + i, 0, 0, 0), base),
                    ),
                    whole(analysis.shape),
                    whole(synthesis.shape),
                    whole(rate.shape),
                ],
                out_specs=pl.BlockSpec((owners, 2, 1, 2, fields, lats_here), lambda i, *_: (0, 0, i, 0, 0, 0)),
            ),
            compiler_params=pltpu.CompilerParams(vmem_limit_bytes=46 * 2**20),
            cost_estimate=pl.CostEstimate(
                flops=size * 16 * modes_count * lat_total * col_count * 4,
                bytes_accessed=size * 2 * (lat_total * col_count + 8 * modes_count * lat_total),
                transcendentals=0,
            ),
        )(
            first_wave[base:base + size],
            start_one[base:base + size],
            start_two[base:base + size],
            parity_arg, part, legendre, analysis, synthesis, rate,
        )
        back = back.reshape(owners, 4 * size, fields, lats_here)
        returned.append(lax.all_to_all(back, ("lat", "lev"), split_axis=0, concat_axis=0, tiled=True))

    total = None
    for chunk in range(chunks):
        size, own = sizes[chunk], returned[chunk]
        if total is not None:
            own, total = lax.optimization_barrier((own, total))
        own = own.reshape(owners, 2, size * 2, -1)
        partner = swap_pair(own, "fld")
        weight = jnp.where(chunk_waves[chunk] == 0, 1.0, 2.0).astype(F32)
        hemisphere = (partner.astype(F32) + sign_own * own.astype(F32)) * weight[:, None, :, None]
        hemisphere = hemisphere.astype(BF16).reshape(owners * 4 * size, -1)
        term = lax.dot_general(
            hemisphere, tables[chunk], (((0,), (0,)), ((), ())), preferred_element_type=F32
        )
        total = term if total is None else total + term
    return total.astype(BF16).reshape(field_count, levels_here, 1, lats_here, lon_count)


def solution(mesh):
    return jax.shard_map(
        local,
        mesh=mesh,
        in_specs=(
            P("member", "lev", "fld", "lat", None),
            P(("lat", "lev"), "fld", None, None),
            P(),
            P(),
            P(),
            P(),
            P(),
        ),
        out_specs=P("member", "lev", "fld", "lat", None),
        check_vma=False,
    )
```
